32 devices in a mesh: xy: 16 (over z, y, x), gz: 2 (over core).
Axes of the slice: x: 2, y: 2, z: 4, core: 2. Of those that a mesh axis runs over, the one named last changes fastest.
Arguments:
- potential_temp: float32 [4, 64, 512], P('gz', 'xy'), may hold values from -6 to 6
- wind_field: float32 [3, 4, 64, 512], P(None, 'gz', 'xy'), may hold values from -0.25 to 0.25
- eddy_diff: float32 [4, 64, 512], P('gz', 'xy'), may hold values from 0.005 to 0.04
- facade_cell: int32 [2, 2048, 128], P('gz', 'xy'), may hold values from 0 to 4095
- tile_send: int32 [2, 2048], P('gz', 'xy'), may hold values from -1 to 127, as said below
- tile_take: int32 [2, 1024], P('gz', 'xy'), may hold values from 0 to 127, as said below
- wall_temp: float32 [2, 1024, 32, 128], P('gz', 'xy'), may hold values from -6 to 6
- wall_class: int32 [2, 1024], P('gz', 'xy'), may hold values from 0 to 3
- wall_inverse: float32 [4, 32, 32], replicated, as said below
- refl_block: bfloat16 [16, 32, 128, 128], P('xy', 'gz'), may hold values from -0.5 to 0.5
- refl_pair: int32 [16, 2, 32], P('xy', None, 'gz'), may hold values from 0 to 127
Outputs:
- temp_next: float32 [4, 64, 512], P('gz', 'xy')
- wall_next: float32 [2, 1024, 32, 128], P('gz', 'xy')
The draws below stay inside these ranges and needn't reach their ends.
Inputs may be any that keep to these rules, and one draw needn't show every extreme that they name: `tile_send`: in each vertical index, each LES device's live slots carry distinct values dest * 8 + c with c below the number of tiles that it sends to owner dest, and at most 8 tiles go from one LES device to one owner; some LES device has all 128 slots live, with 8 tiles to every owner, and empty slots hold -1. `tile_take`: for owner j at vertical index k, the 64 values are exactly the rows src * 8 + c for which LES device src sends a tile with value j * 8 + c, each once; every owner receives exactly 64 tiles. `wall_inverse`: nonnegative entries, diagonally dominant by rows.
All inputs are finite; a program needn't handle non-finite values.
Results may differ from the reference program's by a relative error of at most 0.0014.
Values may be sent and summed in bfloat16 or wider, within the bound.
A program may use at most 64 MiB of HBM per device.

```python
import math
import jax
import jax.numpy as jnp
from jax import lax

CZ = 2
CX = 4
NY = 512
TILE = 128
NODES = 32
NMAT = 4
SUB = 4
OWN = 64
NB = 16
TMAX = 128
CAP = 8
NZ = 4
NX = 64
N_XY = 16
N_GZ = 2


def routing_level(level_key):
    pair_count = N_XY // 2
    order = jax.random.permutation(jax.random.fold_in(level_key, 1), N_XY).astype(jnp.int32)
    at_end = ((order == 0) | (order == N_XY - 1)).astype(jnp.int32)
    order = order[jnp.argsort(at_end * N_XY + jnp.arange(N_XY, dtype=jnp.int32))]
    first_rows = order[0::2]
    second_rows = order[1::2]
    bias = jax.random.randint(jax.random.fold_in(level_key, 2), (pair_count, 1, 1), 250, 751)
    coin = jax.random.randint(jax.random.fold_in(level_key, 3), (pair_count, N_XY, CAP), 0, 1000)
    counts_first = jnp.sum((coin < bias).astype(jnp.int32), axis=2)
    high_col = jax.random.randint(jax.random.fold_in(level_key, 4), (pair_count,), 0, N_XY)
    low_col = (high_col + 1 + jax.random.randint(jax.random.fold_in(level_key, 5), (pair_count,), 0, N_XY - 1)) % N_XY
    columns = jnp.arange(N_XY, dtype=jnp.int32)[None, :]
    counts_first = jnp.where(columns == high_col[:, None], CAP, counts_first)
    counts_first = jnp.where(columns == low_col[:, None], 0, counts_first)
    full_pair = (jnp.arange(pair_count) == 0)[:, None]
    counts_first = jnp.where(full_pair, CAP, counts_first).astype(jnp.int32)
    counts_second = (CAP - counts_first).astype(jnp.int32)
    matrix = jnp.zeros((N_XY, N_XY), jnp.int32).at[first_rows].set(counts_first).at[second_rows].set(counts_second)
    return matrix


def send_level(level_key, matrix):
    cumulative = jnp.cumsum(matrix, axis=1)
    live_count = cumulative[:, -1]
    ranks = jnp.arange(TMAX, dtype=jnp.int32)
    destination = jnp.sum((cumulative[:, None, :] <= ranks[None, :, None]).astype(jnp.int32), axis=2)
    destination = jnp.minimum(destination, N_XY - 1)
    before = jnp.take_along_axis(cumulative - matrix, destination, axis=1)
    place = ranks[None, :] - before
    values = jnp.where(ranks[None, :] < live_count[:, None], destination * CAP + place, -1).astype(jnp.int32)
    slot_keys = jax.random.split(jax.random.fold_in(level_key, 6), N_XY)
    slot_order = jax.vmap(lambda one_key: jax.random.permutation(one_key, TMAX))(slot_keys).astype(jnp.int32)
    device_ids = jnp.arange(N_XY, dtype=jnp.int32)[:, None]
    rows = jnp.zeros((N_XY, TMAX), jnp.int32).at[device_ids, slot_order].set(values)
    return rows.reshape(N_XY * TMAX)


def take_level(level_key, matrix):
    index = jnp.arange(N_XY * CAP, dtype=jnp.int32)
    source = index // CAP
    place = index % CAP
    valid = (place[None, :] < jnp.transpose(matrix)[:, source]).astype(jnp.int32)
    score = (1 - valid) * (N_XY * CAP) + index[None, :]
    chosen = jnp.argsort(score, axis=1)[:, :OWN].astype(jnp.int32)
    home_keys = jax.random.split(jax.random.fold_in(level_key, 7), N_XY)
    home_order = jax.vmap(lambda one_key: jax.random.permutation(one_key, OWN))(home_keys).astype(jnp.int32)
    result = jnp.take_along_axis(chosen, home_order, axis=1)
    return result.reshape(N_XY * OWN).astype(jnp.int32)


def level_lists(key):

    def one_level(level):
        level_key = jax.random.fold_in(key, 1000 + level)
        matrix = routing_level(level_key)
        return (send_level(level_key, matrix), take_level(level_key, matrix))
    return jax.vmap(one_level)(jnp.arange(N_GZ, dtype=jnp.int32))


def draw_tile_send(key, part):
    return level_lists(key)[0]


def draw_tile_take(key, part):
    return level_lists(key)[1]


def draw_wall_inverse(key, part):
    main_part = jax.random.uniform(jax.random.fold_in(key, 11), (NMAT, NODES, NODES), jnp.float32, 0.4, 0.8)
    side_part = jax.random.uniform(jax.random.fold_in(key, 12), (NMAT, NODES, NODES), jnp.float32, 0.0, 0.5 / NODES)
    row_ids = lax.broadcasted_iota(jnp.int32, (NMAT, NODES, NODES), 1)
    col_ids = lax.broadcasted_iota(jnp.int32, (NMAT, NODES, NODES), 2)
    return jnp.where(row_ids == col_ids, main_part, side_part)


def plant(drawn, stream_key, least, top_value):
    extent = drawn.shape
    index_at = [jax.random.randint(jax.random.fold_in(stream_key, axis), (), 0, extent[axis]) for axis in range(len(extent))]
    drawn = drawn.at[tuple(index_at)].set(least)
    longest = extent.index(max(extent))
    index_at[longest] = (index_at[longest] + 1) % extent[longest]
    return drawn.at[tuple(index_at)].set(top_value)


def level_of(key, shape, shards, least, high):
    level, own = 1.0, jax.random.fold_in(key, 6)
    for axis_at, parts in shards:
        draws = jnp.exp(jax.random.uniform(jax.random.fold_in(own, axis_at), (parts,), jnp.float32, least / len(shards), high / len(shards)))
        level = level * jnp.repeat(draws, shape[axis_at] // parts).reshape([-1 if axis == axis_at else 1 for axis in range(len(shape))])
    return level


def gaussian(rng, extent, deviation, reach, pieces=(), kind=jnp.bfloat16):
    array = deviation * jax.random.normal(rng, extent, jnp.float32)
    if pieces:
        array = array * level_of(rng, extent, pieces, -0.22, 0.18)
    return jnp.clip(array, -reach, reach).astype(kind)


def setup_inputs(seed: int = 0) -> dict:
    keys = jax.random.split(jax.random.key(seed), 12)
    potential_temp = gaussian(keys[0], (NZ, NX, NY), 1.0, 6.0, ((0, 2), (1, 16)), jnp.float32)
    wind_field = jnp.clip(jax.random.uniform(keys[1], (3, NZ, NX, NY), jnp.float32, -0.25, 0.25) * level_of(keys[1], (3, NZ, NX, NY), ((1, 2), (2, 16)), -0.4, 0.0), -0.25, 0.25)
    eddy_diff = jnp.clip(jnp.exp(math.log(0.04) - 2.0794415 * jax.random.uniform(keys[2], (NZ, NX, NY), jnp.float32) ** level_of(keys[2], (NZ, NX, NY), ((0, 2), (1, 16)), -0.2, 0.2)), 0.005, 0.04)
    facade_cell = plant(jax.random.randint(keys[3], (N_GZ, N_XY * TMAX, TILE), 0, CZ * CX * NY), jax.random.fold_in(keys[3], 1), 0, (CZ * CX * NY) - 1).astype(jnp.int32)
    tile_send = draw_tile_send(jax.random.fold_in(keys[11], 71), 0)
    tile_take = draw_tile_take(jax.random.fold_in(keys[11], 71), 0)
    wall_temp = gaussian(keys[6], (N_GZ, N_XY * OWN, NODES, TILE), 1.0, 6.0, ((0, 2), (1, 16)), jnp.float32)
    wall_class = plant(jax.random.randint(keys[7], (N_GZ, N_XY * OWN), 0, NMAT), jax.random.fold_in(keys[7], 1), 0, NMAT - 1).astype(jnp.int32)
    wall_inverse = draw_wall_inverse(jax.random.fold_in(keys[11], 71), 0)
    refl_block = gaussian(keys[9], (N_XY, N_GZ * NB, TILE, TILE), TILE ** -0.5, 0.5, ((0, 16), (1, 2)))
    refl_pair = plant(jax.random.randint(keys[10], (N_XY, 2, N_GZ * NB), 0, N_GZ * OWN), jax.random.fold_in(keys[10], 1), 0, (N_GZ * OWN) - 1).astype(jnp.int32)
    return {"potential_temp": potential_temp, "wind_field": wind_field, "eddy_diff": eddy_diff, "facade_cell": facade_cell, "tile_send": tile_send, "tile_take": tile_take, "wall_temp": wall_temp, "wall_class": wall_class, "wall_inverse": wall_inverse, "refl_block": refl_block, "refl_pair": refl_pair}


wall_gain = 0.25
flux_gain = 0.5


def upwind(speed, centre, lower, upper):
    return jnp.maximum(speed, 0.0) * (centre - lower) + jnp.minimum(speed, 0.0) * (upper - centre)


def to_devices(field):
    cell_count = CZ * CX * NY
    return field.reshape(N_GZ, CZ, N_XY, CX, NY).transpose(0, 2, 1, 3, 4).reshape(N_GZ, N_XY, cell_count)


def from_devices(field):
    return field.reshape(N_GZ, N_XY, CZ, CX, NY).transpose(0, 2, 1, 3, 4).reshape(NZ, NX, NY)


def district_sum(inputs):
    blocks, pair_rows, emitted = inputs
    source_emit = emitted[pair_rows[1]].astype(jnp.float32)
    contrib = jnp.einsum("bij,bj->bi", blocks.astype(jnp.float32), source_emit)
    return jnp.zeros((N_GZ * OWN, TILE), jnp.float32).at[pair_rows[0]].add(contrib)


def reference(potential_temp, wind_field, eddy_diff, facade_cell, tile_send, tile_take, wall_temp, wall_class, wall_inverse, refl_block, refl_pair):
    slot_total = N_XY * CAP
    speed_sq = wind_field[0] * wind_field[0] + wind_field[1] * wind_field[1] + wind_field[2] * wind_field[2]
    theta_dev = to_devices(potential_temp)
    speed_dev = to_devices(speed_sq)
    cell_index = facade_cell.reshape(N_GZ, N_XY, TMAX * TILE)
    air_slots = jnp.take_along_axis(theta_dev, cell_index, axis=2).reshape(N_GZ, N_XY, TMAX, TILE)
    coef_slots = 0.5 + 4.0 * jnp.take_along_axis(speed_dev, cell_index, axis=2).reshape(N_GZ, N_XY, TMAX, TILE)
    send_rows = tile_send.reshape(N_GZ, N_XY, TMAX)
    level_ids = jnp.arange(N_GZ, dtype=jnp.int32)[:, None, None]
    device_ids = jnp.arange(N_XY, dtype=jnp.int32)[None, :, None]
    target_rows = jnp.where(send_rows >= 0, send_rows, slot_total)
    empty_box = jnp.zeros((N_GZ, N_XY, slot_total + 1, TILE), potential_temp.dtype)
    air_out = empty_box.at[level_ids, device_ids, target_rows].set(air_slots)[:, :, :slot_total]
    coef_out = empty_box.at[level_ids, device_ids, target_rows].set(coef_slots)[:, :, :slot_total]
    take_rows = tile_take.reshape(N_GZ, N_XY, OWN)
    source_dev = take_rows // CAP
    source_col = take_rows % CAP
    own_air = air_out[level_ids, source_dev, device_ids * CAP + source_col]
    own_coef = coef_out[level_ids, source_dev, device_ids * CAP + source_col]
    wall_state = wall_temp.reshape(N_GZ, N_XY, OWN, NODES, TILE)
    emitted = wall_state[:, :, :, 0, :].astype(jnp.bfloat16)
    district_emit = emitted.transpose(1, 0, 2, 3).reshape(N_XY, N_GZ * OWN, TILE)
    reflected = lax.map(district_sum, (refl_block, refl_pair, district_emit))
    own_rad = reflected.reshape(N_XY, N_GZ, OWN, TILE).transpose(1, 0, 2, 3)
    inverse_tile = wall_inverse[wall_class.reshape(N_GZ, N_XY, OWN)]
    temps = wall_state
    for substep in range(SUB):
        forcing = own_coef * (own_air - temps[:, :, :, 0, :]) + own_rad
        temps = temps.at[:, :, :, 0, :].add(wall_gain * forcing)
        temps = jnp.einsum("kjhab,kjhbf->kjhaf", inverse_tile, temps, precision=lax.Precision.HIGHEST)
    flux_out = own_coef * (temps[:, :, :, 0, :] - own_air)
    back_rows = jnp.zeros((N_GZ, N_XY, slot_total, TILE), potential_temp.dtype)
    back_rows = back_rows.at[level_ids, source_dev, device_ids * CAP + source_col].set(flux_out)
    slot_flux = back_rows[level_ids, device_ids, jnp.maximum(send_rows, 0)]
    slot_flux = jnp.where((send_rows >= 0)[:, :, :, None], slot_flux, 0.0)
    heat_dev = jnp.zeros((N_GZ, N_XY, CZ * CX * NY), potential_temp.dtype)
    heat_dev = heat_dev.at[level_ids, device_ids, cell_index].add(slot_flux.reshape(N_GZ, N_XY, TMAX * TILE))
    heat_cells = from_devices(heat_dev)
    centre = potential_temp
    padded = jnp.pad(centre, ((1, 1), (1, 1), (0, 0)))
    lower_z = padded[:-2, 1:-1]
    upper_z = padded[2:, 1:-1]
    lower_x = padded[1:-1, :-2]
    upper_x = padded[1:-1, 2:]
    lower_y = jnp.roll(centre, 1, axis=2)
    upper_y = jnp.roll(centre, -1, axis=2)
    advect = upwind(wind_field[0], centre, lower_z, upper_z) + upwind(wind_field[1], centre, lower_x, upper_x) + upwind(wind_field[2], centre, lower_y, upper_y)
    laplace = (lower_z + upper_z + lower_x + upper_x + lower_y + upper_y) - 6.0 * centre
    temp_next = centre - advect + eddy_diff * laplace + flux_gain * heat_cells
    return temp_next, temps.reshape(N_GZ, N_XY * OWN, NODES, TILE)
```

```python
import jax
import jax.numpy as jnp
from jax import lax
from jax.experimental import pallas as pl
from jax.experimental.pallas import tpu as pltpu
from jax.sharding import PartitionSpec as P

SUB = 4


wall_gain = 0.25
flux_gain = 0.5


def upwind(speed, centre, lower, upper):
    return jnp.maximum(speed, 0.0) * (centre - lower) + jnp.minimum(speed, 0.0) * (upper - centre)


LANES = 128
HIGH = lax.Precision.HIGHEST
VMEM_LIMIT = 40 * 1024 * 1024


def contract(a, b, dims):
    return lax.dot_general(
        a, b, (dims, ((), ())), precision=HIGH, preferred_element_type=jnp.float32
    )


def slot_matrix(send_ref, total):
    slots = send_ref.shape[1]
    row_ids = lax.broadcasted_iota(jnp.int32, (total, slots), 0)
    return (row_ids == send_ref[...]).astype(jnp.float32)


def lookup_kernel(theta_ref, wind_ref, cell_ref, send_ref, out_ref, coef_ref, found_ref):
    levels, rows, y_cells = theta_ref.shape
    slots, width = found_ref.shape[0], found_ref.shape[1] // 2
    pieces = y_cells // LANES
    w0, w1, w2 = wind_ref[0], wind_ref[1], wind_ref[2]
    coef_ref[...] = 0.5 + 4.0 * (w0 * w0 + w1 * w1 + w2 * w2)

    def group(g, carry):
        start = pl.multiple_of(g * 8, 8)
        cells = cell_ref[0, pl.ds(start, 8), :]
        lane = cells % LANES
        piece = cells // LANES
        air = jnp.zeros((8, width), jnp.float32)
        coef = jnp.zeros((8, width), jnp.float32)
        for b in range(levels * rows * pieces):
            line, j = b // pieces, b % pieces
            z, x = line // rows, line % rows
            cut = slice(j * LANES, (j + 1) * LANES)
            hit = piece == b
            theta_row = jnp.broadcast_to(theta_ref[z, x : x + 1, cut], (8, LANES))
            coef_row = jnp.broadcast_to(coef_ref[z, x : x + 1, cut], (8, LANES))
            air = jnp.where(hit, jnp.take_along_axis(theta_row, lane, axis=1), air)
            coef = jnp.where(hit, jnp.take_along_axis(coef_row, lane, axis=1), coef)
        found_ref[pl.ds(start, 8), :width] = air
        found_ref[pl.ds(start, 8), width:] = coef
        return carry

    lax.fori_loop(0, slots // 8, group, 0)
    count, capacity = out_ref.shape[0], out_ref.shape[1]
    listed = contract(slot_matrix(send_ref, count * capacity), found_ref[...], ((1,), (0,)))
    for j in range(count):
        out_ref[j] = listed[j * capacity : (j + 1) * capacity]


def heat_kernel(
    theta_ref, wind_ref, eddy_ref, cell_ref, send_ref, back_ref,
    low_x_ref, high_x_ref, low_z_ref, high_z_ref, out_ref, rows_ref, flux_ref,
):
    levels, rows, y_cells = theta_ref.shape
    lines, pieces = levels * rows, y_cells // LANES
    slots, width = flux_ref.shape
    count, capacity = back_ref.shape[0], back_ref.shape[1]
    for j in range(count):
        rows_ref[j * capacity : (j + 1) * capacity, :] = back_ref[j]
    flux_ref[...] = contract(
        slot_matrix(send_ref, count * capacity), rows_ref[...], ((0,), (0,))
    )
    step = 8
    row_ids = lax.broadcasted_iota(jnp.int32, (lines * pieces, width), 0)
    lane_ids = lax.broadcasted_iota(jnp.int32, (LANES, width), 0)

    def group(g, total):
        start = pl.multiple_of(g * step, step)
        cells = cell_ref[0, pl.ds(start, step), :]
        flux = flux_ref[pl.ds(start, step), :]
        lane = cells % LANES
        place = (cells % y_cells) // LANES * lines + cells // y_cells
        upper = flux.astype(jnp.bfloat16).astype(jnp.float32)
        lower = flux - upper
        left, right = [], []
        for s in range(step):
            hit = row_ids == place[s : s + 1]
            left.append(
                jnp.concatenate(
                    (jnp.where(hit, upper[s : s + 1], 0.0), jnp.where(hit, lower[s : s + 1], 0.0)), 0
                ).astype(jnp.bfloat16)
            )
            right.append(
                jnp.where(lane_ids == lane[s : s + 1], 1.0, 0.0).astype(jnp.bfloat16)
            )
        return total + lax.dot_general(
            jnp.concatenate(left, 1),
            jnp.concatenate(right, 1),
            (((1,), (1,)), ((), ())),
            preferred_element_type=jnp.float32,
        )

    total = lax.fori_loop(
        0, slots // step, group, jnp.zeros((2 * lines * pieces, LANES), jnp.float32)
    )
    total = total[: lines * pieces] + total[lines * pieces :]
    heat = jnp.concatenate([total[j * lines : (j + 1) * lines] for j in range(pieces)], 1)
    for z in range(levels):
        c = theta_ref[z]
        lower_z = low_z_ref[...] if z == 0 else theta_ref[z - 1]
        upper_z = high_z_ref[...] if z == levels - 1 else theta_ref[z + 1]
        lower_x = jnp.concatenate((low_x_ref[z : z + 1], c[:-1]), 0)
        upper_x = jnp.concatenate((c[1:], high_x_ref[z : z + 1]), 0)
        lower_y = jnp.roll(c, 1, axis=1)
        upper_y = jnp.roll(c, -1, axis=1)
        advect = (
            upwind(wind_ref[0, z], c, lower_z, upper_z)
            + upwind(wind_ref[1, z], c, lower_x, upper_x)
            + upwind(wind_ref[2, z], c, lower_y, upper_y)
        )
        laplace = lower_z + upper_z + lower_x + upper_x + lower_y + upper_y - 6.0 * c
        out_ref[z] = (
            c - advect + eddy_ref[z] * laplace + flux_gain * heat[z * rows : (z + 1) * rows]
        )


def call_lookup(theta, wind, cells, send, count, capacity):
    slots, width = cells.shape[1], cells.shape[2]
    return pl.pallas_call(
        lookup_kernel,
        out_shape=jax.ShapeDtypeStruct((count, capacity, 2 * width), jnp.float32),
        in_specs=[pl.BlockSpec(memory_space=pltpu.VMEM)] * 4,
        out_specs=pl.BlockSpec(memory_space=pltpu.VMEM),
        scratch_shapes=[
            pltpu.VMEM(theta.shape, jnp.float32),
            pltpu.VMEM((slots, 2 * width), jnp.float32),
        ],
        compiler_params=pltpu.CompilerParams(vmem_limit_bytes=VMEM_LIMIT),
        name="lookup",
    )(theta, wind, cells, send)


def call_heat(theta, wind, eddy, cells, send, back, halos):
    slots, width = cells.shape[1], cells.shape[2]
    return pl.pallas_call(
        heat_kernel,
        out_shape=jax.ShapeDtypeStruct(theta.shape, jnp.float32),
        in_specs=[pl.BlockSpec(memory_space=pltpu.VMEM)] * 10,
        out_specs=pl.BlockSpec(memory_space=pltpu.VMEM),
        scratch_shapes=[
            pltpu.VMEM((back.shape[0] * back.shape[1], width), jnp.float32),
            pltpu.VMEM((slots, width), jnp.float32),
        ],
        compiler_params=pltpu.CompilerParams(vmem_limit_bytes=VMEM_LIMIT),
        name="heat",
    )(theta, wind, eddy, cells, send, back, *halos)


def on_device(
    potential_temp,
    wind_field,
    eddy_diff,
    facade_cell,
    tile_send,
    tile_take,
    wall_temp,
    wall_class,
    wall_inverse,
    refl_block,
    refl_pair,
):
    levels, x_rows, y_cells = potential_temp.shape
    tile_slots = facade_cell.shape[1]
    tile_width = facade_cell.shape[2]
    owned = tile_take.shape[1]
    node_count = wall_temp.shape[2]
    xy_count = lax.axis_size("xy")
    capacity = 2 * owned // xy_count
    slot_total = xy_count * capacity
    listed = call_lookup(potential_temp, wind_field, facade_cell, tile_send, xy_count, capacity)
    halos = []
    for axis, dim in (("xy", 1), ("gz", 0)):
        size, length = lax.axis_size(axis), potential_temp.shape[dim]
        up = [(i, i + 1) for i in range(size - 1)]
        down = [(j, i) for i, j in up]
        halos.append(lax.ppermute(lax.index_in_dim(potential_temp, length - 1, dim, False), axis, up))
        halos.append(lax.ppermute(lax.index_in_dim(potential_temp, 0, dim, False), axis, down))
    received = lax.all_to_all(listed, "xy", split_axis=0, concat_axis=0, tiled=True)
    received = received.reshape(slot_total, 2 * tile_width)
    take_rows = tile_take.reshape(owned)
    own_both = received[take_rows]
    own_air, own_coef = own_both[:, :tile_width], own_both[:, tile_width:]
    wall_state = wall_temp.reshape(owned, node_count, tile_width)
    emitted = wall_state[:, 0, :].astype(jnp.bfloat16)
    district = lax.all_gather(emitted, "gz", axis=0, tiled=True)
    blocks = refl_block[0]
    pair_rows = refl_pair[0]
    source_emit = district[pair_rows[1]]
    contrib = jnp.einsum("bij,bj->bi", blocks, source_emit, preferred_element_type=jnp.float32)
    targets = pair_rows[0]
    district_rows = lax.axis_size("gz") * owned
    row_ids = lax.iota(jnp.int32, district_rows)
    one_hot = (row_ids[:, None] == targets[None, :]).astype(jnp.float32)
    whole = lax.psum(
        jnp.dot(
            one_hot, contrib, precision=lax.Precision.HIGHEST, preferred_element_type=jnp.float32
        ).astype(jnp.bfloat16),
        "gz",
    ).astype(jnp.float32)
    own_rad = lax.dynamic_slice_in_dim(whole, lax.axis_index("gz") * owned, owned, 0)
    class_ids = lax.broadcasted_iota(jnp.int32, (owned, wall_inverse.shape[0]), 1)
    class_hot = (wall_class.reshape(owned)[:, None] == class_ids).astype(jnp.float32)
    inverse_tile = jnp.einsum(
        "tc,cab->tab", class_hot, wall_inverse, precision=lax.Precision.HIGHEST
    )
    temps = wall_state
    for substep in range(SUB):
        forcing = own_coef * (own_air - temps[:, 0, :]) + own_rad
        temps = temps.at[:, 0, :].add(wall_gain * forcing)
        temps = jnp.einsum("tab,tbf->taf", inverse_tile, temps, precision=lax.Precision.HIGHEST)
    flux_out = own_coef * (temps[:, 0, :] - own_air)
    back_rows = jnp.zeros((slot_total, tile_width), jnp.float32).at[take_rows].set(flux_out)
    returned = lax.all_to_all(
        back_rows.reshape(xy_count, capacity, tile_width), "xy", split_axis=0, concat_axis=0, tiled=True
    )
    temp_next = call_heat(
        potential_temp, wind_field, eddy_diff, facade_cell, tile_send, returned, halos
    )
    return (temp_next, temps.reshape(1, owned, node_count, tile_width))


def solution(mesh):
    in_specs = (
        P("gz", "xy", None),
        P(None, "gz", "xy", None),
        P("gz", "xy", None),
        P("gz", "xy", None),
        P("gz", "xy"),
        P("gz", "xy"),
        P("gz", "xy", None, None),
        P("gz", "xy"),
        P(),
        P("xy", "gz", None, None),
        P("xy", None, "gz"),
    )
    out_specs = (P("gz", "xy", None), P("gz", "xy", None, None))
    return jax.shard_map(
        on_device, mesh=mesh, in_specs=in_specs, out_specs=out_specs, check_vma=False
    )
```

```python
import functools

import jax
import jax.numpy as jnp
from jax import lax
from jax.experimental import pallas as pl
from jax.experimental.pallas import tpu as pltpu
from jax.sharding import PartitionSpec as P

SUB = 4


wall_gain = 0.25
flux_gain = 0.5


def upwind(speed, centre, lower, upper):
    return jnp.maximum(speed, 0.0) * (centre - lower) + jnp.minimum(speed, 0.0) * (upper - centre)


LANES = 128
HIGH = lax.Precision.HIGHEST
VMEM_LIMIT = 40 * 1024 * 1024


def contract(a, b, dims):
    return lax.dot_general(
        a, b, (dims, ((), ())), precision=HIGH, preferred_element_type=jnp.float32
    )


def slot_matrix(send_ref, total):
    slots = send_ref.shape[1]
    row_ids = lax.broadcasted_iota(jnp.int32, (total, slots), 0)
    return (row_ids == send_ref[...]).astype(jnp.float32)


def lookup_kernel(theta_ref, wind_ref, cell_ref, send_ref, out_ref, coef_ref, found_ref):
    levels, rows, y_cells = theta_ref.shape
    slots, width = found_ref.shape[0], found_ref.shape[1] // 2
    pieces = y_cells // LANES
    w0, w1, w2 = wind_ref[0], wind_ref[1], wind_ref[2]
    coef_ref[...] = 0.5 + 4.0 * (w0 * w0 + w1 * w1 + w2 * w2)

    def group(g, carry):
        start = pl.multiple_of(g * 8, 8)
        cells = cell_ref[0, pl.ds(start, 8), :]
        lane = cells % LANES
        piece = cells // LANES
        air = jnp.zeros((8, width), jnp.float32)
        coef = jnp.zeros((8, width), jnp.float32)
        for b in range(levels * rows * pieces):
            line, j = b // pieces, b % pieces
            z, x = line // rows, line % rows
            cut = slice(j * LANES, (j + 1) * LANES)
            hit = piece == b
            theta_row = jnp.broadcast_to(theta_ref[z, x : x + 1, cut], (8, LANES))
            coef_row = jnp.broadcast_to(coef_ref[z, x : x + 1, cut], (8, LANES))
            air = jnp.where(hit, jnp.take_along_axis(theta_row, lane, axis=1), air)
            coef = jnp.where(hit, jnp.take_along_axis(coef_row, lane, axis=1), coef)
        found_ref[pl.ds(start, 8), :width] = air
        found_ref[pl.ds(start, 8), width:] = coef
        return carry

    lax.fori_loop(0, slots // 8, group, 0)
    count, capacity = out_ref.shape[0], out_ref.shape[1]
    listed = contract(slot_matrix(send_ref, count * capacity), found_ref[...], ((1,), (0,)))
    for j in range(count):
        out_ref[j] = listed[j * capacity : (j + 1) * capacity]


def heat_kernel(
    theta_ref, wind_ref, eddy_ref, cell_ref, send_ref, back_ref,
    low_x_ref, high_x_ref, low_z_ref, high_z_ref, out_ref, rows_ref, flux_ref,
):
    levels, rows, y_cells = theta_ref.shape
    lines, pieces = levels * rows, y_cells // LANES
    slots, width = flux_ref.shape
    count, capacity = back_ref.shape[0], back_ref.shape[1]
    for j in range(count):
        rows_ref[j * capacity : (j + 1) * capacity, :] = back_ref[j]
    flux_ref[...] = contract(
        slot_matrix(send_ref, count * capacity), rows_ref[...], ((0,), (0,))
    )
    step = 8
    row_ids = lax.broadcasted_iota(jnp.int32, (lines * pieces, width), 0)
    lane_ids = lax.broadcasted_iota(jnp.int32, (LANES, width), 0)

    def group(g, total):
        start = pl.multiple_of(g * step, step)
        cells = cell_ref[0, pl.ds(start, step), :]
        flux = flux_ref[pl.ds(start, step), :]
        lane = cells % LANES
        place = (cells % y_cells) // LANES * lines + cells // y_cells
        upper = flux.astype(jnp.bfloat16).astype(jnp.float32)
        lower = flux - upper
        left, right = [], []
        for s in range(step):
            hit = row_ids == place[s : s + 1]
            left.append(
                jnp.concatenate(
                    (jnp.where(hit, upper[s : s + 1], 0.0), jnp.where(hit, lower[s : s + 1], 0.0)), 0
                ).astype(jnp.bfloat16)
            )
            right.append(
                jnp.where(lane_ids == lane[s : s + 1], 1.0, 0.0).astype(jnp.bfloat16)
            )
        return total + lax.dot_general(
            jnp.concatenate(left, 1),
            jnp.concatenate(right, 1),
            (((1,), (1,)), ((), ())),
            preferred_element_type=jnp.float32,
        )

    total = lax.fori_loop(
        0, slots // step, group, jnp.zeros((2 * lines * pieces, LANES), jnp.float32)
    )
    total = total[: lines * pieces] + total[lines * pieces :]
    heat = jnp.concatenate([total[j * lines : (j + 1) * lines] for j in range(pieces)], 1)
    for z in range(levels):
        c = theta_ref[z]
        lower_z = low_z_ref[...] if z == 0 else theta_ref[z - 1]
        upper_z = high_z_ref[...] if z == levels - 1 else theta_ref[z + 1]
        lower_x = jnp.concatenate((low_x_ref[z : z + 1], c[:-1]), 0)
        upper_x = jnp.concatenate((c[1:], high_x_ref[z : z + 1]), 0)
        lower_y = jnp.roll(c, 1, axis=1)
        upper_y = jnp.roll(c, -1, axis=1)
        advect = (
            upwind(wind_ref[0, z], c, lower_z, upper_z)
            + upwind(wind_ref[1, z], c, lower_x, upper_x)
            + upwind(wind_ref[2, z], c, lower_y, upper_y)
        )
        laplace = lower_z + upper_z + lower_x + upper_x + lower_y + upper_y - 6.0 * c
        out_ref[z] = (
            c - advect + eddy_ref[z] * laplace + flux_gain * heat[z * rows : (z + 1) * rows]
        )


def call_lookup(theta, wind, cells, send, count, capacity):
    slots, width = cells.shape[1], cells.shape[2]
    return pl.pallas_call(
        lookup_kernel,
        out_shape=jax.ShapeDtypeStruct((count, capacity, 2 * width), jnp.float32),
        in_specs=[pl.BlockSpec(memory_space=pltpu.VMEM)] * 4,
        out_specs=pl.BlockSpec(memory_space=pltpu.VMEM),
        scratch_shapes=[
            pltpu.VMEM(theta.shape, jnp.float32),
            pltpu.VMEM((slots, 2 * width), jnp.float32),
        ],
        compiler_params=pltpu.CompilerParams(vmem_limit_bytes=VMEM_LIMIT),
        name="lookup",
    )(theta, wind, cells, send)


def call_heat(theta, wind, eddy, cells, send, back, halos):
    slots, width = cells.shape[1], cells.shape[2]
    return pl.pallas_call(
        heat_kernel,
        out_shape=jax.ShapeDtypeStruct(theta.shape, jnp.float32),
        in_specs=[pl.BlockSpec(memory_space=pltpu.VMEM)] * 10,
        out_specs=pl.BlockSpec(memory_space=pltpu.VMEM),
        scratch_shapes=[
            pltpu.VMEM((back.shape[0] * back.shape[1], width), jnp.float32),
            pltpu.VMEM((slots, width), jnp.float32),
        ],
        compiler_params=pltpu.CompilerParams(vmem_limit_bytes=VMEM_LIMIT),
        name="heat",
    )(theta, wind, eddy, cells, send, back, *halos)


def wall_kernel(
    count, groups,
    listed_ref, theta_ref, take_ref, class_ref, wall_ref, inverse_ref, block_ref, pair_ref,
    wall_out, back_out, low_x_out, high_x_out, low_z_out, high_z_out,
    recv_ref, flat_ref, edge_ref, edge_got, side_got, district_ref, part_ref, own_part_ref,
    part_got, matrix_ref, kick_ref, rows_ref, diag_ref, gain_ref, back_ref, back_got,
    edge_sems, side_sems, emit_sems, part_sems, list_sems, back_sems,
):
    me, level = lax.axis_index("xy"), lax.axis_index("gz")
    levels, x_rows = theta_ref.shape[0], theta_ref.shape[1]
    capacity = listed_ref.shape[1]
    owned, nodes, width = wall_ref.shape[1], wall_ref.shape[2], wall_ref.shape[3]
    classes = inverse_ref.shape[0]

    barrier = pltpu.get_barrier_semaphore()
    for k in range(1, count):
        pl.semaphore_signal(
            barrier, inc=1, device_id={"xy": lax.rem(me + k, count)},
            device_id_type=pl.DeviceIdType.MESH,
        )
    for k in range(1, groups):
        pl.semaphore_signal(
            barrier, inc=1, device_id={"gz": lax.rem(level + k, groups)},
            device_id_type=pl.DeviceIdType.MESH,
        )
    pl.semaphore_wait(barrier, count + groups - 2)

    def send(src, dst, sems, at, axis, peer):
        copy = pltpu.make_async_remote_copy(
            src_ref=src, dst_ref=dst, send_sem=sems.at[0, at], recv_sem=sems.at[1, at],
            device_id={axis: peer}, device_id_type=pl.DeviceIdType.MESH,
        )
        copy.start()
        return copy

    list_copies = []
    for k in range(1, count):
        peer = lax.rem(me + k, count)
        list_copies.append(
            send(listed_ref.at[peer], recv_ref.at[me], list_sems, k - 1, "xy", peer)
        )
    first = wall_ref[0, :, 0, :]
    district_ref[level] = first.astype(jnp.bfloat16)
    emit_copies = []
    for k in range(1, groups):
        peer = lax.rem(level + k, groups)
        emit_copies.append(
            send(district_ref.at[level], district_ref.at[level], emit_sems, k - 1, "gz", peer)
        )
    edge_ref[0] = theta_ref[:, x_rows - 1, :]
    edge_ref[1] = theta_ref[:, 0, :]
    next_x, last_x = lax.rem(me + 1, count), lax.rem(me + count - 1, count)
    next_z, last_z = lax.rem(level + 1, groups), lax.rem(level + groups - 1, groups)
    halo_copies = [
        send(edge_ref.at[0], edge_got.at[0], edge_sems, 0, "xy", next_x),
        send(edge_ref.at[1], edge_got.at[1], edge_sems, 1, "xy", last_x),
        send(theta_ref.at[levels - 1], side_got.at[0], side_sems, 0, "gz", next_z),
        send(theta_ref.at[0], side_got.at[1], side_sems, 1, "gz", last_z),
    ]
    recv_ref[me] = listed_ref[me]

    for c in range(classes):
        a1 = inverse_ref[c]
        a2 = contract(a1, a1, ((1,), (0,)))
        a3 = contract(a2, a1, ((1,), (0,)))
        a4 = contract(a2, a2, ((1,), (0,)))
        for p, power in enumerate((a1, a2, a3, a4)):
            kick_ref[c, p] = jnp.broadcast_to(power[:, :1], (nodes, width))
        stacked = jnp.concatenate((a4, a1[:1], a2[:1], a3[:1], jnp.zeros((5, nodes))), 0)
        upper = stacked.astype(jnp.bfloat16).astype(jnp.float32)
        matrix_ref[c] = jnp.concatenate((upper, upper, stacked - upper), 1)

    for copy in emit_copies:
        copy.wait()
    total = groups * owned
    district = district_ref[...].astype(jnp.float32).reshape(total, width)
    blocks = block_ref.shape[1]
    row_ids = lax.broadcasted_iota(jnp.int32, (total, blocks), 0)
    source_hot = (row_ids == pair_ref[0, 1:2, :]).astype(jnp.float32)
    target_hot = (row_ids == pair_ref[0, 0:1, :]).astype(jnp.float32)
    source = contract(source_hot, district, ((0,), (0,)))
    contrib = jnp.concatenate(
        [
            lax.dot_general(
                source[b : b + 1].astype(jnp.bfloat16), block_ref[0, b],
                (((1,), (1,)), ((), ())), preferred_element_type=jnp.float32,
            )
            for b in range(blocks)
        ],
        0,
    )
    part = contract(target_hot, contrib, ((1,), (0,)))
    for g in range(groups):
        own_part_ref[g] = part[g * owned : (g + 1) * owned]
        part_ref[g] = part[g * owned : (g + 1) * owned].astype(jnp.bfloat16)
    part_copies = []
    for k in range(1, groups):
        peer = lax.rem(level + k, groups)
        part_copies.append(
            send(part_ref.at[peer], part_got.at[k - 1], part_sems, k - 1, "gz", peer)
        )

    def advance(h, carry):
        t = wall_ref[0, h]
        kind = class_ref[0, h]
        upper = t.astype(jnp.bfloat16)
        lower = (t - upper.astype(jnp.float32)).astype(jnp.bfloat16)
        got = jnp.dot(
            matrix_ref[kind].astype(jnp.bfloat16),
            jnp.concatenate((upper, lower, upper), 0),
            preferred_element_type=jnp.float32,
        )
        wall_out[0, h] = got[:nodes]
        rows_ref[3, pl.ds(h, 1)] = got[:1]
        for p in range(3):
            rows_ref[p, pl.ds(h, 1)] = got[nodes + p : nodes + p + 1]
        for p in range(SUB):
            diag_ref[p, pl.ds(h, 1)] = kick_ref[kind, p, :1, :]
        return carry

    lax.fori_loop(0, owned, advance, 0, unroll=4)

    for copy in part_copies:
        copy.wait()
    rad = own_part_ref[level]
    for k in range(groups - 1):
        rad = rad + part_got[k].astype(jnp.float32)
    for copy in list_copies:
        copy.wait()
    for j in range(count):
        flat_ref[j * capacity : (j + 1) * capacity, :] = recv_ref[j]
    take_hot = (
        lax.broadcasted_iota(jnp.int32, (count * capacity, owned), 0) == take_ref[...]
    ).astype(jnp.float32)
    both = contract(take_hot, flat_ref[...], ((0,), (0,)))
    air, coef = both[:, :width], both[:, width:]
    surface, gains = first, []
    for step in range(SUB):
        gains.append(wall_gain * (coef * (air - surface) + rad))
        gain_ref[step] = gains[step]
        surface = rows_ref[step]
        for q in range(step + 1):
            surface = surface + diag_ref[step - q] * gains[q]
    back = contract(take_hot, coef * (surface - air), ((1,), (0,)))
    for j in range(count):
        back_ref[j] = back[j * capacity : (j + 1) * capacity]
    back_copies = []
    for k in range(1, count):
        peer = lax.rem(me + k, count)
        back_copies.append(
            send(back_ref.at[peer], back_got.at[me], back_sems, k - 1, "xy", peer)
        )
    back_got[me] = back_ref[me]

    def finish(h, carry):
        kind = class_ref[0, h]
        t = wall_out[0, h]
        for q in range(SUB):
            t = t + kick_ref[kind, SUB - 1 - q] * gain_ref[q, pl.ds(h, 1)]
        wall_out[0, h] = t
        return carry

    lax.fori_loop(0, owned, finish, 0, unroll=4)

    for copy in halo_copies:
        copy.wait()
    low_x_out[...] = edge_got[0] * (me > 0).astype(jnp.float32)
    high_x_out[...] = edge_got[1] * (me < count - 1).astype(jnp.float32)
    low_z_out[...] = side_got[0] * (level > 0).astype(jnp.float32)
    high_z_out[...] = side_got[1] * (level < groups - 1).astype(jnp.float32)
    for copy in back_copies:
        copy.wait()
    back_out[...] = back_got[...]


def call_wall(listed, theta, take, kinds, wall, inverse, blocks, pairs):
    count, groups = lax.axis_size("xy"), lax.axis_size("gz")
    capacity = listed.shape[1]
    owned, nodes, width = wall.shape[1:]
    levels, x_rows, y_cells = theta.shape
    classes = inverse.shape[0]
    f32, bf16 = jnp.float32, jnp.bfloat16
    vmem = pl.BlockSpec(memory_space=pltpu.VMEM)
    smem = pl.BlockSpec(memory_space=pltpu.SMEM)
    x_side = jax.ShapeDtypeStruct((levels, y_cells), f32)
    z_side = jax.ShapeDtypeStruct((x_rows, y_cells), f32)

    def pairs_of(n):
        return pltpu.SemaphoreType.DMA((2, n))

    return pl.pallas_call(
        functools.partial(wall_kernel, count, groups),
        out_shape=(
            jax.ShapeDtypeStruct(wall.shape, f32),
            jax.ShapeDtypeStruct((count, capacity, width), f32),
            x_side, x_side, z_side, z_side,
        ),
        in_specs=[vmem, vmem, vmem, smem, vmem, vmem, vmem, vmem],
        out_specs=(vmem,) * 6,
        scratch_shapes=[
            pltpu.VMEM(listed.shape, f32),
            pltpu.VMEM((count * capacity, 2 * width), f32),
            pltpu.VMEM((2, levels, y_cells), f32),
            pltpu.VMEM((2, levels, y_cells), f32),
            pltpu.VMEM((2, x_rows, y_cells), f32),
            pltpu.VMEM((groups, owned, width), bf16),
            pltpu.VMEM((groups, owned, width), bf16),
            pltpu.VMEM((groups, owned, width), f32),
            pltpu.VMEM((groups - 1, owned, width), bf16),
            pltpu.VMEM((classes, nodes + 8, 3 * nodes), f32),
            pltpu.VMEM((classes, SUB, nodes, width), f32),
            pltpu.VMEM((SUB, owned, width), f32),
            pltpu.VMEM((SUB, owned, width), f32),
            pltpu.VMEM((SUB, owned, width), f32),
            pltpu.VMEM((count, capacity, width), f32),
            pltpu.VMEM((count, capacity, width), f32),
            pairs_of(2), pairs_of(2), pairs_of(groups - 1), pairs_of(groups - 1),
            pairs_of(count - 1), pairs_of(count - 1),
        ],
        compiler_params=pltpu.CompilerParams(
            collective_id=0, has_side_effects=True, vmem_limit_bytes=VMEM_LIMIT
        ),
        name="wall",
    )(listed, theta, take, kinds, wall, inverse, blocks, pairs)


def on_device(
    potential_temp,
    wind_field,
    eddy_diff,
    facade_cell,
    tile_send,
    tile_take,
    wall_temp,
    wall_class,
    wall_inverse,
    refl_block,
    refl_pair,
):
    xy_count = lax.axis_size("xy")
    capacity = 2 * tile_take.shape[1] // xy_count
    listed = call_lookup(potential_temp, wind_field, facade_cell, tile_send, xy_count, capacity)
    wall_next, returned, *halos = call_wall(
        listed, potential_temp, tile_take, wall_class, wall_temp, wall_inverse, refl_block, refl_pair
    )
    temp_next = call_heat(
        potential_temp, wind_field, eddy_diff, facade_cell, tile_send, returned, halos
    )
    return (temp_next, wall_next)


def solution(mesh):
    in_specs = (
        P("gz", "xy", None),
        P(None, "gz", "xy", None),
        P("gz", "xy", None),
        P("gz", "xy", None),
        P("gz", "xy"),
        P("gz", "xy"),
        P("gz", "xy", None, None),
        P("gz", "xy"),
        P(),
        P("xy", "gz", None, None),
        P("xy", None, "gz"),
    )
    out_specs = (P("gz", "xy", None), P("gz", "xy", None, None))
    return jax.shard_map(
        on_device, mesh=mesh, in_specs=in_specs, out_specs=out_specs, check_vma=False
    )
```

```python
import functools

import jax
import jax.numpy as jnp
from jax import lax
from jax.experimental import pallas as pl
from jax.experimental.pallas import tpu as pltpu
from jax.sharding import PartitionSpec as P

SUB = 4


wall_gain = 0.25
flux_gain = 0.5


def upwind(speed, centre, lower, upper):
    return jnp.maximum(speed, 0.0) * (centre - lower) + jnp.minimum(speed, 0.0) * (upper - centre)


LANES = 128
HIGH = lax.Precision.HIGHEST
LOOKUP_VMEM, HEAT_VMEM, WALL_VMEM = (n * 1024 * 1024 for n in (60, 60, 60))


def contract(a, b, dims):
    return lax.dot_general(
        a, b, (dims, ((), ())), precision=HIGH, preferred_element_type=jnp.float32
    )


def slot_matrix(send_ref, total):
    slots = send_ref.shape[1]
    row_ids = lax.broadcasted_iota(jnp.int32, (total, slots), 0)
    return (row_ids == send_ref[...]).astype(jnp.float32)


def fetch(pairs, sems):
    copies = [
        pltpu.make_async_copy(src, dst, sems.at[n]) for n, (src, dst) in enumerate(pairs)
    ]
    for copy in copies:
        copy.start()
    return copies


def lookup_kernel(
    theta_hbm, wind_hbm, cell_hbm, send_hbm, out_ref,
    theta_ref, wind_ref, cell_ref, send_ref, coef_ref, found_ref, sems,
):
    copies = fetch(
        (
            (theta_hbm, theta_ref), (wind_hbm, wind_ref), (cell_hbm, cell_ref),
            (send_hbm, send_ref),
        ),
        sems,
    )
    for copy in copies:
        copy.wait()
    levels, rows, y_cells = theta_ref.shape
    slots, width = found_ref.shape[0], found_ref.shape[1] // 2
    pieces = y_cells // LANES
    w0, w1, w2 = wind_ref[0], wind_ref[1], wind_ref[2]
    coef_ref[...] = 0.5 + 4.0 * (w0 * w0 + w1 * w1 + w2 * w2)

    def group(g, carry):
        start = pl.multiple_of(g * 8, 8)
        cells = cell_ref[0, pl.ds(start, 8), :]
        lane = cells % LANES
        piece = cells // LANES
        air = jnp.zeros((8, width), jnp.float32)
        coef = jnp.zeros((8, width), jnp.float32)
        for b in range(levels * rows * pieces):
            line, j = b // pieces, b % pieces
            z, x = line // rows, line % rows
            cut = slice(j * LANES, (j + 1) * LANES)
            hit = piece == b
            theta_row = jnp.broadcast_to(theta_ref[z, x : x + 1, cut], (8, LANES))
            coef_row = jnp.broadcast_to(coef_ref[z, x : x + 1, cut], (8, LANES))
            air = jnp.where(hit, jnp.take_along_axis(theta_row, lane, axis=1), air)
            coef = jnp.where(hit, jnp.take_along_axis(coef_row, lane, axis=1), coef)
        found_ref[pl.ds(start, 8), :width] = air
        found_ref[pl.ds(start, 8), width:] = coef
        return carry

    lax.fori_loop(0, slots // 8, group, 0)
    count, capacity = out_ref.shape[0], out_ref.shape[1]
    listed = contract(slot_matrix(send_ref, count * capacity), found_ref[...], ((1,), (0,)))
    for j in range(count):
        out_ref[j] = listed[j * capacity : (j + 1) * capacity]


def heat_kernel(
    theta_ref, wind_ref, eddy_ref, cell_ref, send_ref, back_ref,
    low_x_ref, high_x_ref, low_z_ref, high_z_ref, wall_ref, out_ref, wall_out,
    rows_ref, flux_ref, sem,
):
    wall_copy = pltpu.make_async_copy(wall_ref, wall_out, sem)
    wall_copy.start()
    levels, rows, y_cells = theta_ref.shape
    lines, pieces = levels * rows, y_cells // LANES
    slots, width = flux_ref.shape
    count, capacity = back_ref.shape[0], back_ref.shape[1]
    for j in range(count):
        rows_ref[j * capacity : (j + 1) * capacity, :] = back_ref[j]
    flux_ref[...] = contract(
        slot_matrix(send_ref, count * capacity), rows_ref[...], ((0,), (0,))
    )
    step = 8
    row_ids = lax.broadcasted_iota(jnp.int32, (lines * pieces, width), 0)
    lane_ids = lax.broadcasted_iota(jnp.int32, (LANES, width), 0)

    def group(g, total):
        start = pl.multiple_of(g * step, step)
        cells = cell_ref[0, pl.ds(start, step), :]
        flux = flux_ref[pl.ds(start, step), :]
        lane = cells % LANES
        place = (cells % y_cells) // LANES * lines + cells // y_cells
        upper = flux.astype(jnp.bfloat16).astype(jnp.float32)
        lower = flux - upper
        left, right = [], []
        for s in range(step):
            hit = row_ids == place[s : s + 1]
            left.append(
                jnp.concatenate(
                    (jnp.where(hit, upper[s : s + 1], 0.0), jnp.where(hit, lower[s : s + 1], 0.0)), 0
                ).astype(jnp.bfloat16)
            )
            right.append(
                jnp.where(lane_ids == lane[s : s + 1], 1.0, 0.0).astype(jnp.bfloat16)
            )
        return total + lax.dot_general(
            jnp.concatenate(left, 1),
            jnp.concatenate(right, 1),
            (((1,), (1,)), ((), ())),
            preferred_element_type=jnp.float32,
        )

    total = lax.fori_loop(
        0, slots // step, group, jnp.zeros((2 * lines * pieces, LANES), jnp.float32)
    )
    total = total[: lines * pieces] + total[lines * pieces :]
    heat = jnp.concatenate([total[j * lines : (j + 1) * lines] for j in range(pieces)], 1)
    for z in range(levels):
        c = theta_ref[z]
        lower_z = low_z_ref[...] if z == 0 else theta_ref[z - 1]
        upper_z = high_z_ref[...] if z == levels - 1 else theta_ref[z + 1]
        lower_x = jnp.concatenate((low_x_ref[z : z + 1], c[:-1]), 0)
        upper_x = jnp.concatenate((c[1:], high_x_ref[z : z + 1]), 0)
        lower_y = jnp.roll(c, 1, axis=1)
        upper_y = jnp.roll(c, -1, axis=1)
        advect = (
            upwind(wind_ref[0, z], c, lower_z, upper_z)
            + upwind(wind_ref[1, z], c, lower_x, upper_x)
            + upwind(wind_ref[2, z], c, lower_y, upper_y)
        )
        laplace = lower_z + upper_z + lower_x + upper_x + lower_y + upper_y - 6.0 * c
        out_ref[z] = (
            c - advect + eddy_ref[z] * laplace + flux_gain * heat[z * rows : (z + 1) * rows]
        )
    wall_copy.wait()


def call_lookup(theta, wind, cells, send, count, capacity):
    slots, width = cells.shape[1], cells.shape[2]
    return pl.pallas_call(
        lookup_kernel,
        out_shape=jax.ShapeDtypeStruct((count, capacity, 2 * width), jnp.float32),
        in_specs=[pl.BlockSpec(memory_space=pltpu.HBM)] * 4,
        out_specs=pl.BlockSpec(memory_space=pltpu.VMEM),
        scratch_shapes=[
            pltpu.VMEM(theta.shape, jnp.float32),
            pltpu.VMEM(wind.shape, jnp.float32),
            pltpu.VMEM(cells.shape, jnp.int32),
            pltpu.VMEM(send.shape, jnp.int32),
            pltpu.VMEM(theta.shape, jnp.float32),
            pltpu.VMEM((slots, 2 * width), jnp.float32),
            pltpu.SemaphoreType.DMA((4,)),
        ],
        compiler_params=pltpu.CompilerParams(vmem_limit_bytes=LOOKUP_VMEM),
        name="lookup",
    )(theta, wind, cells, send)


def call_heat(theta, wind, eddy, cells, send, back, halos, wall):
    slots, width = cells.shape[1], cells.shape[2]
    return pl.pallas_call(
        heat_kernel,
        out_shape=(
            jax.ShapeDtypeStruct(theta.shape, jnp.float32),
            jax.ShapeDtypeStruct(wall.shape, jnp.float32),
        ),
        in_specs=[pl.BlockSpec(memory_space=pltpu.VMEM)] * 10
        + [pl.BlockSpec(memory_space=pl.ANY)],
        out_specs=(
            pl.BlockSpec(memory_space=pltpu.VMEM), pl.BlockSpec(memory_space=pltpu.HBM),
        ),
        scratch_shapes=[
            pltpu.VMEM((back.shape[0] * back.shape[1], width), jnp.float32),
            pltpu.VMEM((slots, width), jnp.float32),
            pltpu.SemaphoreType.DMA(()),
        ],
        compiler_params=pltpu.CompilerParams(vmem_limit_bytes=HEAT_VMEM),
        name="heat",
    )(theta, wind, eddy, cells, send, back, *halos, wall)


def wall_kernel(
    count, groups,
    listed_ref, theta_hbm, take_hbm, class_ref, wall_hbm, inverse_hbm, block_hbm, pair_hbm,
    wall_out, back_out, low_x_out, high_x_out, low_z_out, high_z_out,
    recv_ref, flat_ref, edge_ref, edge_got, side_got, district_ref, part_ref, own_part_ref,
    part_got, matrix_ref, kick_ref, rows_ref, diag_ref, gain_ref, back_ref, back_got,
    edge_sems, side_sems, emit_sems, part_sems, list_sems, back_sems,
    theta_ref, take_ref, wall_ref, inverse_ref, block_ref, pair_ref, fetch_sems,
):
    me, level = lax.axis_index("xy"), lax.axis_index("gz")
    levels, x_rows = theta_ref.shape[0], theta_ref.shape[1]
    capacity = listed_ref.shape[1]
    owned, nodes, width = wall_ref.shape[1], wall_ref.shape[2], wall_ref.shape[3]
    classes = inverse_ref.shape[0]

    fetches = fetch(
        (
            (theta_hbm, theta_ref), (wall_hbm, wall_ref), (inverse_hbm, inverse_ref),
            (take_hbm, take_ref), (pair_hbm, pair_ref), (block_hbm, block_ref),
        ),
        fetch_sems,
    )
    barrier = pltpu.get_barrier_semaphore()
    for k in range(1, count):
        pl.semaphore_signal(
            barrier, inc=1, device_id={"xy": lax.rem(me + k, count)},
            device_id_type=pl.DeviceIdType.MESH,
        )
    for k in range(1, groups):
        pl.semaphore_signal(
            barrier, inc=1, device_id={"gz": lax.rem(level + k, groups)},
            device_id_type=pl.DeviceIdType.MESH,
        )
    pl.semaphore_wait(barrier, count + groups - 2)

    def send(src, dst, sems, at, axis, peer):
        copy = pltpu.make_async_remote_copy(
            src_ref=src, dst_ref=dst, send_sem=sems.at[0, at], recv_sem=sems.at[1, at],
            device_id={axis: peer}, device_id_type=pl.DeviceIdType.MESH,
        )
        copy.start()
        return copy

    list_copies = []
    for k in range(1, count):
        peer = lax.rem(me + k, count)
        list_copies.append(
            send(listed_ref.at[peer], recv_ref.at[me], list_sems, k - 1, "xy", peer)
        )
    for copy in fetches:
        copy.wait()
    first = wall_ref[0, :, 0, :]
    district_ref[level] = first.astype(jnp.bfloat16)
    emit_copies = []
    for k in range(1, groups):
        peer = lax.rem(level + k, groups)
        emit_copies.append(
            send(district_ref.at[level], district_ref.at[level], emit_sems, k - 1, "gz", peer)
        )
    edge_ref[0] = theta_ref[:, x_rows - 1, :]
    edge_ref[1] = theta_ref[:, 0, :]
    next_x, last_x = lax.rem(me + 1, count), lax.rem(me + count - 1, count)
    next_z, last_z = lax.rem(level + 1, groups), lax.rem(level + groups - 1, groups)
    halo_copies = [
        send(edge_ref.at[0], edge_got.at[0], edge_sems, 0, "xy", next_x),
        send(edge_ref.at[1], edge_got.at[1], edge_sems, 1, "xy", last_x),
        send(theta_ref.at[levels - 1], side_got.at[0], side_sems, 0, "gz", next_z),
        send(theta_ref.at[0], side_got.at[1], side_sems, 1, "gz", last_z),
    ]
    recv_ref[me] = listed_ref[me]

    for c in range(classes):
        a1 = inverse_ref[c]
        a2 = contract(a1, a1, ((1,), (0,)))
        a3 = contract(a2, a1, ((1,), (0,)))
        a4 = contract(a2, a2, ((1,), (0,)))
        for p, power in enumerate((a1, a2, a3, a4)):
            kick_ref[c, p] = jnp.broadcast_to(power[:, :1], (nodes, width))
        stacked = jnp.concatenate((a4, a1[:1], a2[:1], a3[:1], jnp.zeros((5, nodes))), 0)
        upper = stacked.astype(jnp.bfloat16).astype(jnp.float32)
        matrix_ref[c] = jnp.concatenate((upper, upper, stacked - upper), 1)

    for copy in emit_copies:
        copy.wait()
    total = groups * owned
    district = district_ref[...].astype(jnp.float32).reshape(total, width)
    blocks = block_ref.shape[1]
    row_ids = lax.broadcasted_iota(jnp.int32, (total, blocks), 0)
    source_hot = (row_ids == pair_ref[0, 1:2, :]).astype(jnp.float32)
    target_hot = (row_ids == pair_ref[0, 0:1, :]).astype(jnp.float32)
    source = contract(source_hot, district, ((0,), (0,)))
    contrib = jnp.concatenate(
        [
            lax.dot_general(
                source[b : b + 1].astype(jnp.bfloat16), block_ref[0, b],
                (((1,), (1,)), ((), ())), preferred_element_type=jnp.float32,
            )
            for b in range(blocks)
        ],
        0,
    )
    part = contract(target_hot, contrib, ((1,), (0,)))
    for g in range(groups):
        own_part_ref[g] = part[g * owned : (g + 1) * owned]
        part_ref[g] = part[g * owned : (g + 1) * owned].astype(jnp.bfloat16)
    part_copies = []
    for k in range(1, groups):
        peer = lax.rem(level + k, groups)
        part_copies.append(
            send(part_ref.at[peer], part_got.at[k - 1], part_sems, k - 1, "gz", peer)
        )

    def advance(h, carry):
        t = wall_ref[0, h]
        kind = class_ref[0, h]
        upper = t.astype(jnp.bfloat16)
        lower = (t - upper.astype(jnp.float32)).astype(jnp.bfloat16)
        got = jnp.dot(
            matrix_ref[kind].astype(jnp.bfloat16),
            jnp.concatenate((upper, lower, upper), 0),
            preferred_element_type=jnp.float32,
        )
        wall_out[0, h] = got[:nodes]
        rows_ref[3, pl.ds(h, 1)] = got[:1]
        for p in range(3):
            rows_ref[p, pl.ds(h, 1)] = got[nodes + p : nodes + p + 1]
        for p in range(SUB):
            diag_ref[p, pl.ds(h, 1)] = kick_ref[kind, p, :1, :]
        return carry

    lax.fori_loop(0, owned, advance, 0, unroll=4)

    for copy in part_copies:
        copy.wait()
    rad = own_part_ref[level]
    for k in range(groups - 1):
        rad = rad + part_got[k].astype(jnp.float32)
    for copy in list_copies:
        copy.wait()
    for j in range(count):
        flat_ref[j * capacity : (j + 1) * capacity, :] = recv_ref[j]
    take_hot = (
        lax.broadcasted_iota(jnp.int32, (count * capacity, owned), 0) == take_ref[...]
    ).astype(jnp.float32)
    both = contract(take_hot, flat_ref[...], ((0,), (0,)))
    air, coef = both[:, :width], both[:, width:]
    surface, gains = first, []
    for step in range(SUB):
        gains.append(wall_gain * (coef * (air - surface) + rad))
        gain_ref[step] = gains[step]
        surface = rows_ref[step]
        for q in range(step + 1):
            surface = surface + diag_ref[step - q] * gains[q]
    back = contract(take_hot, coef * (surface - air), ((1,), (0,)))
    for j in range(count):
        back_ref[j] = back[j * capacity : (j + 1) * capacity]
    back_copies = []
    for k in range(1, count):
        peer = lax.rem(me + k, count)
        back_copies.append(
            send(back_ref.at[peer], back_got.at[me], back_sems, k - 1, "xy", peer)
        )
    back_got[me] = back_ref[me]

    def finish(h, carry):
        kind = class_ref[0, h]
        t = wall_out[0, h]
        for q in range(SUB):
            t = t + kick_ref[kind, SUB - 1 - q] * gain_ref[q, pl.ds(h, 1)]
        wall_out[0, h] = t
        return carry

    lax.fori_loop(0, owned, finish, 0, unroll=4)

    for copy in halo_copies:
        copy.wait()
    low_x_out[...] = edge_got[0] * (me > 0).astype(jnp.float32)
    high_x_out[...] = edge_got[1] * (me < count - 1).astype(jnp.float32)
    low_z_out[...] = side_got[0] * (level > 0).astype(jnp.float32)
    high_z_out[...] = side_got[1] * (level < groups - 1).astype(jnp.float32)
    for copy in back_copies:
        copy.wait()
    back_out[...] = back_got[...]


def call_wall(listed, theta, take, kinds, wall, inverse, blocks, pairs):
    count, groups = lax.axis_size("xy"), lax.axis_size("gz")
    capacity = listed.shape[1]
    owned, nodes, width = wall.shape[1:]
    levels, x_rows, y_cells = theta.shape
    classes = inverse.shape[0]
    f32, bf16 = jnp.float32, jnp.bfloat16
    vmem = pl.BlockSpec(memory_space=pltpu.VMEM)
    hbm = pl.BlockSpec(memory_space=pltpu.HBM)
    smem = pl.BlockSpec(memory_space=pltpu.SMEM)
    x_side = jax.ShapeDtypeStruct((levels, y_cells), f32)
    z_side = jax.ShapeDtypeStruct((x_rows, y_cells), f32)

    def pairs_of(n):
        return pltpu.SemaphoreType.DMA((2, n))

    return pl.pallas_call(
        functools.partial(wall_kernel, count, groups),
        out_shape=(
            jax.ShapeDtypeStruct(wall.shape, f32),
            jax.ShapeDtypeStruct((count, capacity, width), f32),
            x_side, x_side, z_side, z_side,
        ),
        in_specs=[vmem, hbm, hbm, smem, hbm, hbm, hbm, hbm],
        out_specs=(vmem,) * 6,
        scratch_shapes=[
            pltpu.VMEM(listed.shape, f32),
            pltpu.VMEM((count * capacity, 2 * width), f32),
            pltpu.VMEM((2, levels, y_cells), f32),
            pltpu.VMEM((2, levels, y_cells), f32),
            pltpu.VMEM((2, x_rows, y_cells), f32),
            pltpu.VMEM((groups, owned, width), bf16),
            pltpu.VMEM((groups, owned, width), bf16),
            pltpu.VMEM((groups, owned, width), f32),
            pltpu.VMEM((groups - 1, owned, width), bf16),
            pltpu.VMEM((classes, nodes + 8, 3 * nodes), f32),
            pltpu.VMEM((classes, SUB, nodes, width), f32),
            pltpu.VMEM((SUB, owned, width), f32),
            pltpu.VMEM((SUB, owned, width), f32),
            pltpu.VMEM((SUB, owned, width), f32),
            pltpu.VMEM((count, capacity, width), f32),
            pltpu.VMEM((count, capacity, width), f32),
            pairs_of(2), pairs_of(2), pairs_of(groups - 1), pairs_of(groups - 1),
            pairs_of(count - 1), pairs_of(count - 1),
            *(pltpu.VMEM(a.shape, a.dtype) for a in (theta, take, wall, inverse, blocks, pairs)),
            pltpu.SemaphoreType.DMA((6,)),
        ],
        compiler_params=pltpu.CompilerParams(
            collective_id=0, has_side_effects=True, vmem_limit_bytes=WALL_VMEM
        ),
        name="wall",
    )(listed, theta, take, kinds, wall, inverse, blocks, pairs)


def on_device(
    potential_temp,
    wind_field,
    eddy_diff,
    facade_cell,
    tile_send,
    tile_take,
    wall_temp,
    wall_class,
    wall_inverse,
    refl_block,
    refl_pair,
):
    xy_count = lax.axis_size("xy")
    capacity = 2 * tile_take.shape[1] // xy_count
    listed = call_lookup(potential_temp, wind_field, facade_cell, tile_send, xy_count, capacity)
    wall_done, returned, *halos = call_wall(
        listed, potential_temp, tile_take, wall_class, wall_temp, wall_inverse, refl_block, refl_pair
    )
    return call_heat(
        potential_temp, wind_field, eddy_diff, facade_cell, tile_send, returned, halos, wall_done
    )


def solution(mesh):
    in_specs = (
        P("gz", "xy", None),
        P(None, "gz", "xy", None),
        P("gz", "xy", None),
        P("gz", "xy", None),
        P("gz", "xy"),
        P("gz", "xy"),
        P("gz", "xy", None, None),
        P("gz", "xy"),
        P(),
        P("xy", "gz", None, None),
        P("xy", None, "gz"),
    )
    out_specs = (P("gz", "xy", None), P("gz", "xy", None, None))
    return jax.shard_map(
        on_device, mesh=mesh, in_specs=in_specs, out_specs=out_specs, check_vma=False
    )
```

```python
import functools

import jax
import jax.numpy as jnp
from jax import lax
from jax.experimental import pallas as pl
from jax.experimental.pallas import tpu as pltpu
from jax.sharding import PartitionSpec as P

SUB = 4


wall_gain = 0.25
flux_gain = 0.5


def upwind(speed, centre, lower, upper):
    return jnp.maximum(speed, 0.0) * (centre - lower) + jnp.minimum(speed, 0.0) * (upper - centre)


LANES = 128
HIGH = lax.Precision.HIGHEST
LOOKUP_VMEM, HEAT_VMEM, WALL_VMEM = (n * 1024 * 1024 for n in (60, 60, 60))


def contract(a, b, dims):
    return lax.dot_general(
        a, b, (dims, ((), ())), precision=HIGH, preferred_element_type=jnp.float32
    )


def slot_matrix(send_ref, total):
    slots = send_ref.shape[1]
    row_ids = lax.broadcasted_iota(jnp.int32, (total, slots), 0)
    return (row_ids == send_ref[...]).astype(jnp.float32)


def fetch(pairs, sems):
    copies = [
        pltpu.make_async_copy(src, dst, sems.at[n]) for n, (src, dst) in enumerate(pairs)
    ]
    for copy in copies:
        copy.start()
    return copies


def lookup_kernel(
    theta_hbm, wind_hbm, cell_hbm, send_hbm, out_ref,
    theta_ref, wind_ref, cell_ref, send_ref, coef_ref, found_ref, sems,
):
    copies = fetch(
        (
            (theta_hbm, theta_ref), (wind_hbm, wind_ref), (cell_hbm, cell_ref),
            (send_hbm, send_ref),
        ),
        sems,
    )
    for copy in copies:
        copy.wait()
    levels, rows, y_cells = theta_ref.shape
    slots, width = found_ref.shape[0], found_ref.shape[1] // 2
    pieces = y_cells // LANES
    w0, w1, w2 = wind_ref[0], wind_ref[1], wind_ref[2]
    coef_ref[...] = 0.5 + 4.0 * (w0 * w0 + w1 * w1 + w2 * w2)

    def group(g, carry):
        start = pl.multiple_of(g * 8, 8)
        cells = cell_ref[0, pl.ds(start, 8), :]
        lane = cells % LANES
        piece = cells // LANES
        air = jnp.zeros((8, width), jnp.float32)
        coef = jnp.zeros((8, width), jnp.float32)
        for b in range(levels * rows * pieces):
            line, j = b // pieces, b % pieces
            z, x = line // rows, line % rows
            cut = slice(j * LANES, (j + 1) * LANES)
            hit = piece == b
            theta_row = jnp.broadcast_to(theta_ref[z, x : x + 1, cut], (8, LANES))
            coef_row = jnp.broadcast_to(coef_ref[z, x : x + 1, cut], (8, LANES))
            air = jnp.where(hit, jnp.take_along_axis(theta_row, lane, axis=1), air)
            coef = jnp.where(hit, jnp.take_along_axis(coef_row, lane, axis=1), coef)
        found_ref[pl.ds(start, 8), :width] = air
        found_ref[pl.ds(start, 8), width:] = coef
        return carry

    lax.fori_loop(0, slots // 8, group, 0)
    count, capacity = out_ref.shape[0], out_ref.shape[1]
    listed = contract(slot_matrix(send_ref, count * capacity), found_ref[...], ((1,), (0,)))
    for j in range(count):
        out_ref[j] = listed[j * capacity : (j + 1) * capacity]


def heat_kernel(
    theta_ref, wind_ref, eddy_ref, cell_ref, send_ref, back_ref,
    low_x_ref, high_x_ref, low_z_ref, high_z_ref, out_ref,
    rows_ref, flux_ref,
):
    levels, rows, y_cells = theta_ref.shape
    lines, pieces = levels * rows, y_cells // LANES
    slots, width = flux_ref.shape
    count, capacity = back_ref.shape[0], back_ref.shape[1]
    for j in range(count):
        rows_ref[j * capacity : (j + 1) * capacity, :] = back_ref[j]
    flux_ref[...] = contract(
        slot_matrix(send_ref, count * capacity), rows_ref[...], ((0,), (0,))
    )
    step = 8
    row_ids = lax.broadcasted_iota(jnp.int32, (lines * pieces, width), 0)
    lane_ids = lax.broadcasted_iota(jnp.int32, (LANES, width), 0)

    def group(g, total):
        start = pl.multiple_of(g * step, step)
        cells = cell_ref[0, pl.ds(start, step), :]
        flux = flux_ref[pl.ds(start, step), :]
        lane = cells % LANES
        place = (cells % y_cells) // LANES * lines + cells // y_cells
        upper = flux.astype(jnp.bfloat16).astype(jnp.float32)
        lower = flux - upper
        left, right = [], []
        for s in range(step):
            hit = row_ids == place[s : s + 1]
            left.append(
                jnp.concatenate(
                    (jnp.where(hit, upper[s : s + 1], 0.0), jnp.where(hit, lower[s : s + 1], 0.0)), 0
                ).astype(jnp.bfloat16)
            )
            right.append(
                jnp.where(lane_ids == lane[s : s + 1], 1.0, 0.0).astype(jnp.bfloat16)
            )
        return total + lax.dot_general(
            jnp.concatenate(left, 1),
            jnp.concatenate(right, 1),
            (((1,), (1,)), ((), ())),
            preferred_element_type=jnp.float32,
        )

    total = lax.fori_loop(
        0, slots // step, group, jnp.zeros((2 * lines * pieces, LANES), jnp.float32)
    )
    total = total[: lines * pieces] + total[lines * pieces :]
    heat = jnp.concatenate([total[j * lines : (j + 1) * lines] for j in range(pieces)], 1)
    for z in range(levels):
        c = theta_ref[z]
        lower_z = low_z_ref[...] if z == 0 else theta_ref[z - 1]
        upper_z = high_z_ref[...] if z == levels - 1 else theta_ref[z + 1]
        lower_x = jnp.concatenate((low_x_ref[z : z + 1], c[:-1]), 0)
        upper_x = jnp.concatenate((c[1:], high_x_ref[z : z + 1]), 0)
        lower_y = jnp.roll(c, 1, axis=1)
        upper_y = jnp.roll(c, -1, axis=1)
        advect = (
            upwind(wind_ref[0, z], c, lower_z, upper_z)
            + upwind(wind_ref[1, z], c, lower_x, upper_x)
            + upwind(wind_ref[2, z], c, lower_y, upper_y)
        )
        laplace = lower_z + upper_z + lower_x + upper_x + lower_y + upper_y - 6.0 * c
        out_ref[z] = (
            c - advect + eddy_ref[z] * laplace + flux_gain * heat[z * rows : (z + 1) * rows]
        )


def call_lookup(theta, wind, cells, send, count, capacity):
    slots, width = cells.shape[1], cells.shape[2]
    return pl.pallas_call(
        lookup_kernel,
        out_shape=jax.ShapeDtypeStruct((count, capacity, 2 * width), jnp.float32),
        in_specs=[pl.BlockSpec(memory_space=pltpu.HBM)] * 4,
        out_specs=pl.BlockSpec(memory_space=pltpu.VMEM),
        scratch_shapes=[
            pltpu.VMEM(theta.shape, jnp.float32),
            pltpu.VMEM(wind.shape, jnp.float32),
            pltpu.VMEM(cells.shape, jnp.int32),
            pltpu.VMEM(send.shape, jnp.int32),
            pltpu.VMEM(theta.shape, jnp.float32),
            pltpu.VMEM((slots, 2 * width), jnp.float32),
            pltpu.SemaphoreType.DMA((4,)),
        ],
        compiler_params=pltpu.CompilerParams(vmem_limit_bytes=LOOKUP_VMEM),
        name="lookup",
    )(theta, wind, cells, send)


def call_heat(theta, wind, eddy, cells, send, back, halos):
    slots, width = cells.shape[1], cells.shape[2]
    return pl.pallas_call(
        heat_kernel,
        out_shape=jax.ShapeDtypeStruct(theta.shape, jnp.float32),
        in_specs=[pl.BlockSpec(memory_space=pltpu.VMEM)] * 10,
        out_specs=pl.BlockSpec(memory_space=pltpu.VMEM),
        scratch_shapes=[
            pltpu.VMEM((back.shape[0] * back.shape[1], width), jnp.float32),
            pltpu.VMEM((slots, width), jnp.float32),
        ],
        compiler_params=pltpu.CompilerParams(vmem_limit_bytes=HEAT_VMEM),
        name="heat",
    )(theta, wind, eddy, cells, send, back, *halos)


def wall_kernel(
    count, groups,
    listed_ref, theta_hbm, take_hbm, class_ref, wall_hbm, inverse_hbm, block_hbm, pair_hbm,
    wall_out, back_out, low_x_out, high_x_out, low_z_out, high_z_out,
    recv_ref, flat_ref, edge_ref, edge_got, side_got, district_ref, part_ref, own_part_ref,
    part_got, matrix_ref, kick_ref, rows_ref, diag_ref, gain_ref, back_ref, back_got,
    edge_sems, side_sems, emit_sems, part_sems, list_sems, back_sems,
    theta_ref, take_ref, wall_ref, inverse_ref, block_ref, pair_ref, fetch_sems,
):
    me, level = lax.axis_index("xy"), lax.axis_index("gz")
    levels, x_rows = theta_ref.shape[0], theta_ref.shape[1]
    capacity = listed_ref.shape[1]
    owned, nodes, width = wall_ref.shape[1], wall_ref.shape[2], wall_ref.shape[3]
    classes = inverse_ref.shape[0]

    fetches = fetch(
        (
            (theta_hbm, theta_ref), (wall_hbm, wall_ref), (inverse_hbm, inverse_ref),
            (take_hbm, take_ref), (pair_hbm, pair_ref), (block_hbm, block_ref),
        ),
        fetch_sems,
    )
    barrier = pltpu.get_barrier_semaphore()
    for k in range(1, count):
        pl.semaphore_signal(
            barrier, inc=1, device_id={"xy": lax.rem(me + k, count)},
            device_id_type=pl.DeviceIdType.MESH,
        )
    for k in range(1, groups):
        pl.semaphore_signal(
            barrier, inc=1, device_id={"gz": lax.rem(level + k, groups)},
            device_id_type=pl.DeviceIdType.MESH,
        )
    pl.semaphore_wait(barrier, count + groups - 2)

    def send(src, dst, sems, at, axis, peer):
        copy = pltpu.make_async_remote_copy(
            src_ref=src, dst_ref=dst, send_sem=sems.at[0, at], recv_sem=sems.at[1, at],
            device_id={axis: peer}, device_id_type=pl.DeviceIdType.MESH,
        )
        copy.start()
        return copy

    list_copies = []
    for k in range(1, count):
        peer = lax.rem(me + k, count)
        list_copies.append(
            send(listed_ref.at[peer], recv_ref.at[me], list_sems, k - 1, "xy", peer)
        )
    for copy in fetches:
        copy.wait()
    first = wall_ref[0, :, 0, :]
    district_ref[level] = first.astype(jnp.bfloat16)
    emit_copies = []
    for k in range(1, groups):
        peer = lax.rem(level + k, groups)
        emit_copies.append(
            send(district_ref.at[level], district_ref.at[level], emit_sems, k - 1, "gz", peer)
        )
    edge_ref[0] = theta_ref[:, x_rows - 1, :]
    edge_ref[1] = theta_ref[:, 0, :]
    next_x, last_x = lax.rem(me + 1, count), lax.rem(me + count - 1, count)
    next_z, last_z = lax.rem(level + 1, groups), lax.rem(level + groups - 1, groups)
    halo_copies = [
        send(edge_ref.at[0], edge_got.at[0], edge_sems, 0, "xy", next_x),
        send(edge_ref.at[1], edge_got.at[1], edge_sems, 1, "xy", last_x),
        send(theta_ref.at[levels - 1], side_got.at[0], side_sems, 0, "gz", next_z),
        send(theta_ref.at[0], side_got.at[1], side_sems, 1, "gz", last_z),
    ]
    recv_ref[me] = listed_ref[me]

    for c in range(classes):
        a1 = inverse_ref[c]
        a2 = contract(a1, a1, ((1,), (0,)))
        a3 = contract(a2, a1, ((1,), (0,)))
        a4 = contract(a2, a2, ((1,), (0,)))
        for p, power in enumerate((a1, a2, a3, a4)):
            kick_ref[c, p] = jnp.broadcast_to(power[:, :1], (nodes, width))
        stacked = jnp.concatenate((a4, a1[:1], a2[:1], a3[:1], jnp.zeros((5, nodes))), 0)
        upper = stacked.astype(jnp.bfloat16).astype(jnp.float32)
        matrix_ref[c] = jnp.concatenate((upper, upper, stacked - upper), 1)

    for copy in emit_copies:
        copy.wait()
    total = groups * owned
    district = district_ref[...].astype(jnp.float32).reshape(total, width)
    blocks = block_ref.shape[1]
    row_ids = lax.broadcasted_iota(jnp.int32, (total, blocks), 0)
    source_hot = (row_ids == pair_ref[0, 1:2, :]).astype(jnp.float32)
    target_hot = (row_ids == pair_ref[0, 0:1, :]).astype(jnp.float32)
    source = contract(source_hot, district, ((0,), (0,)))
    contrib = jnp.concatenate(
        [
            lax.dot_general(
                source[b : b + 1].astype(jnp.bfloat16), block_ref[0, b],
                (((1,), (1,)), ((), ())), preferred_element_type=jnp.float32,
            )
            for b in range(blocks)
        ],
        0,
    )
    part = contract(target_hot, contrib, ((1,), (0,)))
    for g in range(groups):
        own_part_ref[g] = part[g * owned : (g + 1) * owned]
        part_ref[g] = part[g * owned : (g + 1) * owned].astype(jnp.bfloat16)
    part_copies = []
    for k in range(1, groups):
        peer = lax.rem(level + k, groups)
        part_copies.append(
            send(part_ref.at[peer], part_got.at[k - 1], part_sems, k - 1, "gz", peer)
        )

    def advance(h, carry):
        t = wall_ref[0, h]
        kind = class_ref[0, h]
        upper = t.astype(jnp.bfloat16)
        lower = (t - upper.astype(jnp.float32)).astype(jnp.bfloat16)
        got = jnp.dot(
            matrix_ref[kind].astype(jnp.bfloat16),
            jnp.concatenate((upper, lower, upper), 0),
            preferred_element_type=jnp.float32,
        )
        wall_out[0, h] = got[:nodes]
        rows_ref[3, pl.ds(h, 1)] = got[:1]
        for p in range(3):
            rows_ref[p, pl.ds(h, 1)] = got[nodes + p : nodes + p + 1]
        for p in range(SUB):
            diag_ref[p, pl.ds(h, 1)] = kick_ref[kind, p, :1, :]
        return carry

    lax.fori_loop(0, owned, advance, 0, unroll=4)

    for copy in part_copies:
        copy.wait()
    rad = own_part_ref[level]
    for k in range(groups - 1):
        rad = rad + part_got[k].astype(jnp.float32)
    for copy in list_copies:
        copy.wait()
    for j in range(count):
        flat_ref[j * capacity : (j + 1) * capacity, :] = recv_ref[j]
    take_hot = (
        lax.broadcasted_iota(jnp.int32, (count * capacity, owned), 0) == take_ref[...]
    ).astype(jnp.float32)
    both = contract(take_hot, flat_ref[...], ((0,), (0,)))
    air, coef = both[:, :width], both[:, width:]
    surface, gains = first, []
    for step in range(SUB):
        gains.append(wall_gain * (coef * (air - surface) + rad))
        gain_ref[step] = gains[step]
        surface = rows_ref[step]
        for q in range(step + 1):
            surface = surface + diag_ref[step - q] * gains[q]
    back = contract(take_hot, coef * (surface - air), ((1,), (0,)))
    for j in range(count):
        back_ref[j] = back[j * capacity : (j + 1) * capacity]
    back_copies = []
    for k in range(1, count):
        peer = lax.rem(me + k, count)
        back_copies.append(
            send(back_ref.at[peer], back_got.at[me], back_sems, k - 1, "xy", peer)
        )
    back_got[me] = back_ref[me]

    def finish(h, carry):
        kind = class_ref[0, h]
        t = wall_out[0, h]
        for q in range(SUB):
            t = t + kick_ref[kind, SUB - 1 - q] * gain_ref[q, pl.ds(h, 1)]
        wall_out[0, h] = t
        return carry

    lax.fori_loop(0, owned, finish, 0, unroll=4)

    for copy in halo_copies:
        copy.wait()
    low_x_out[...] = edge_got[0] * (me > 0).astype(jnp.float32)
    high_x_out[...] = edge_got[1] * (me < count - 1).astype(jnp.float32)
    low_z_out[...] = side_got[0] * (level > 0).astype(jnp.float32)
    high_z_out[...] = side_got[1] * (level < groups - 1).astype(jnp.float32)
    for copy in back_copies:
        copy.wait()
    back_out[...] = back_got[...]


def call_wall(listed, theta, take, kinds, wall, inverse, blocks, pairs):
    count, groups = lax.axis_size("xy"), lax.axis_size("gz")
    capacity = listed.shape[1]
    owned, nodes, width = wall.shape[1:]
    levels, x_rows, y_cells = theta.shape
    classes = inverse.shape[0]
    f32, bf16 = jnp.float32, jnp.bfloat16
    vmem = pl.BlockSpec(memory_space=pltpu.VMEM)
    hbm = pl.BlockSpec(memory_space=pltpu.HBM)
    smem = pl.BlockSpec(memory_space=pltpu.SMEM)
    x_side = jax.ShapeDtypeStruct((levels, y_cells), f32)
    z_side = jax.ShapeDtypeStruct((x_rows, y_cells), f32)

    def pairs_of(n):
        return pltpu.SemaphoreType.DMA((2, n))

    return pl.pallas_call(
        functools.partial(wall_kernel, count, groups),
        out_shape=(
            jax.ShapeDtypeStruct(wall.shape, f32),
            jax.ShapeDtypeStruct((count, capacity, width), f32),
            x_side, x_side, z_side, z_side,
        ),
        in_specs=[vmem, hbm, hbm, smem, hbm, hbm, hbm, hbm],
        out_specs=(vmem,) * 6,
        scratch_shapes=[
            pltpu.VMEM(listed.shape, f32),
            pltpu.VMEM((count * capacity, 2 * width), f32),
            pltpu.VMEM((2, levels, y_cells), f32),
            pltpu.VMEM((2, levels, y_cells), f32),
            pltpu.VMEM((2, x_rows, y_cells), f32),
            pltpu.VMEM((groups, owned, width), bf16),
            pltpu.VMEM((groups, owned, width), bf16),
            pltpu.VMEM((groups, owned, width), f32),
            pltpu.VMEM((groups - 1, owned, width), bf16),
            pltpu.VMEM((classes, nodes + 8, 3 * nodes), f32),
            pltpu.VMEM((classes, SUB, nodes, width), f32),
            pltpu.VMEM((SUB, owned, width), f32),
            pltpu.VMEM((SUB, owned, width), f32),
            pltpu.VMEM((SUB, owned, width), f32),
            pltpu.VMEM((count, capacity, width), f32),
            pltpu.VMEM((count, capacity, width), f32),
            pairs_of(2), pairs_of(2), pairs_of(groups - 1), pairs_of(groups - 1),
            pairs_of(count - 1), pairs_of(count - 1),
            *(pltpu.VMEM(a.shape, a.dtype) for a in (theta, take, wall, inverse, blocks, pairs)),
            pltpu.SemaphoreType.DMA((6,)),
        ],
        compiler_params=pltpu.CompilerParams(
            collective_id=0, has_side_effects=True, vmem_limit_bytes=WALL_VMEM
        ),
        name="wall",
    )(listed, theta, take, kinds, wall, inverse, blocks, pairs)


def on_device(
    potential_temp,
    wind_field,
    eddy_diff,
    facade_cell,
    tile_send,
    tile_take,
    wall_temp,
    wall_class,
    wall_inverse,
    refl_block,
    refl_pair,
):
    xy_count = lax.axis_size("xy")
    capacity = 2 * tile_take.shape[1] // xy_count
    listed = call_lookup(potential_temp, wind_field, facade_cell, tile_send, xy_count, capacity)
    wall_next, returned, *halos = call_wall(
        listed, potential_temp, tile_take, wall_class, wall_temp, wall_inverse, refl_block, refl_pair
    )
    temp_next = call_heat(
        potential_temp, wind_field, eddy_diff, facade_cell, tile_send, returned, halos
    )
    return (temp_next, wall_next)


def solution(mesh):
    in_specs = (
        P("gz", "xy", None),
        P(None, "gz", "xy", None),
        P("gz", "xy", None),
        P("gz", "xy", None),
        P("gz", "xy"),
        P("gz", "xy"),
        P("gz", "xy", None, None),
        P("gz", "xy"),
        P(),
        P("xy", "gz", None, None),
        P("xy", None, "gz"),
    )
    out_specs = (P("gz", "xy", None), P("gz", "xy", None, None))
    return jax.shard_map(
        on_device, mesh=mesh, in_specs=in_specs, out_specs=out_specs, check_vma=False
    )
```
